32 devices in a mesh: row: 8 (over z, core), col: 4 (over y, x).
Axes of the slice: x: 2, y: 2, z: 4, core: 2. Of those that a mesh axis runs over, the one named last changes fastest.
Arguments:
- amplitudes: bfloat16 [4096, 4096], P('row', 'col'), may hold values from -6 to 6
- integrals: bfloat16 [4096, 4096], P('col', 'row'), may hold values from -0.125 to 0.125
- amp_occupancy: int32 [32, 32], P('row', 'col'), may hold values 0 or 1
- int_occupancy: int32 [32, 32], P('col', 'row'), may hold values 0 or 1
- owner_map: int32 [32], replicated, may hold values from 0 to 31, each once
Outputs:
- residual: bfloat16 [4096, 4096], P('row', 'col')
The draws below stay inside these ranges and needn't reach their ends.
Inputs may be any that keep to these rules, and one draw needn't show every extreme that they name: `owner_map`: each tile number appears once.
All inputs are finite; a program needn't handle non-finite values. No bound on the sum of `amp_occupancy` or of `int_occupancy` on one device may be relied on, other than what follows from the above.
Results may differ from the reference program's by a relative error of at most 0.014.
Values may be sent and summed in bfloat16 or wider, within the bound.
A program may use at most 64 MiB of HBM per device.

```python
import jax
import jax.numpy as jnp
from jax import lax

TILE = 128
KD = 1024
NJ = 4096
ROWS_ALL = 4096
K_ALL = 4096
NT = 32


def plant(result, stream_key, low, high):
    place = [jax.random.randint(jax.random.fold_in(stream_key, axis), (), 0, length) for axis, length in enumerate(result.shape)]
    widest = result.shape.index(max(result.shape))
    beside = place[:widest] + [(place[widest] + 1) % result.shape[widest]] + place[widest + 1:]
    return result.at[tuple(place)].set(low).at[tuple(beside)].set(high)


def spiked(entries, stream_key, source, target, blocks, factor):
    def block_of(axis_at):
        return (jnp.arange(entries.shape[axis_at]) // (entries.shape[axis_at] // blocks)).reshape((-1,) + (1,) * (entries.ndim - 1 - axis_at))

    one_side = jax.random.permutation(stream_key, blocks)[block_of(target)]
    second = (block_of(target) + blocks // 2) % blocks
    return jnp.where((block_of(source) == one_side) | (block_of(source) == second), factor * entries, entries)


def level_of(own_key, dims, split, low, top_value):
    loudness = 1.0
    for position, parts in split:
        steps = jax.random.uniform(jax.random.fold_in(jax.random.fold_in(own_key, 6), position), (parts,), jnp.float32, low / len(split), top_value / len(split))
        loudness = loudness * jnp.repeat(jnp.exp(steps), dims[position] // parts).reshape((-1,) + (1,) * (len(dims) - 1 - position))
    return loudness


def noise(key, extent, width, most, pieces=(), kind=jnp.bfloat16):
    array = jax.random.normal(key, extent, jnp.float32) * width
    if len(pieces) > 0:
        array = level_of(key, extent, pieces, -0.22, 0.18) * array
    return jnp.clip(array, min=-most, max=most).astype(kind)


def bell_draw_with(key, extent, spread, reach, pieces, heavy, kind=jnp.bfloat16):
    array = spread * jax.random.normal(key, extent, jnp.float32)
    if pieces:
        array = array * level_of(key, extent, pieces, -0.22, 0.18)
    return jnp.clip(spiked(array, jax.random.fold_in(key, 3), *heavy), -reach, reach).astype(kind)


def setup_inputs(seed: int = 0) -> dict:
    key_of = jax.random.split(jax.random.key(seed), 6)
    amplitudes = noise(key_of[0], (ROWS_ALL, K_ALL), 1.0, 6.0, ((0, 8), (1, 4)))
    integrals = bell_draw_with(key_of[1], (K_ALL, NJ), K_ALL ** -0.5, 0.125, ((0, 4), (1, 8)), (0, 1, 8, 2.0))
    amp_occupancy = plant((jax.random.randint(key_of[2], (ROWS_ALL // TILE, K_ALL // TILE), 0, 3) < 2).astype(jnp.int32), jax.random.fold_in(key_of[2], 1), 0, 1)
    int_occupancy = plant((jax.random.randint(key_of[3], (K_ALL // TILE, NT), 0, 3) < 2).astype(jnp.int32), jax.random.fold_in(key_of[3], 1), 0, 1)
    owner_map = jax.random.permutation(key_of[4], NT).astype(jnp.int32)
    return dict(amplitudes=amplitudes, integrals=integrals, amp_occupancy=amp_occupancy, int_occupancy=int_occupancy, owner_map=owner_map)


def mask_tiles(matrix, occupancy):
    nrow, ncolumn = matrix.shape
    blocks = matrix.reshape(nrow // TILE, TILE, ncolumn // TILE, TILE)
    return (blocks * occupancy[:, None, :, None].astype(jnp.bfloat16)).reshape(nrow, ncolumn)


def reference(amplitudes, integrals, amp_occupancy, int_occupancy, owner_map):
    masked_amp = mask_tiles(amplitudes, amp_occupancy)
    masked_int = mask_tiles(integrals, int_occupancy)
    kall = masked_int.shape[0]
    ordered = masked_int.reshape(kall, NT, TILE)[:, owner_map, :].reshape(kall, NJ)
    nblock = kall // KD

    def accumulate(total, index):
        start = (index * KD).astype(jnp.int32)
        left = lax.dynamic_slice_in_dim(masked_amp, start, KD, 1)
        right = lax.dynamic_slice_in_dim(ordered, start, KD, 0)
        part = jnp.dot(left, right, preferred_element_type=jnp.float32).astype(jnp.bfloat16)
        part = lax.optimization_barrier(part)
        return total + part.astype(jnp.float32), None

    start_total = jnp.zeros((masked_amp.shape[0], NJ), jnp.float32)
    total, unused = lax.scan(accumulate, start_total, jnp.arange(nblock, dtype=jnp.int32))
    return total.astype(jnp.bfloat16)
```

```python
import functools

import jax
import jax.numpy as jnp
from jax import lax
from jax.experimental import pallas as pl
from jax.experimental.pallas import tpu as pltpu
from jax.sharding import PartitionSpec as P

TILE = 128
CORES = 2
MESH = pl.DeviceIdType.MESH


def flip(value, mask):
    bit, out = 1, value
    while bit <= mask:
        if mask & bit:
            out = out + bit - 2 * bit * (lax.rem(value // bit, 2))
        bit *= 2
    return out


def orders(ncol):
    bits = [1 << i for i in range(ncol.bit_length() - 1)]
    return (bits, bits[::-1])


def first_stage(offset, order):
    for stage, bit in enumerate(order):
        if offset & bit:
            return stage
    return None


def kernel(nrow, ncol, amp_occ, int_occ, owner, amp, integ, out,
           masked, gath, part, landed, recv, right_send, left_send, twin_send, col_send, col_recv):
    nz = nrow // CORES
    row, col = lax.axis_index("row"), lax.axis_index("col")
    z, core = row // CORES, lax.rem(row, CORES)
    twin = z * CORES + (CORES - 1) - core
    has_left, has_right = z > 0, z < nz - 1
    tiles = integ.shape[1] // TILE
    ktiles = integ.shape[0] // TILE
    nrows = amp.shape[0]
    half = nrows // 2
    width = out.shape[1]
    per_col = width // TILE
    order = orders(ncol)

    barrier = pltpu.get_barrier_semaphore()
    pl.semaphore_signal(barrier, inc=1, device_id={"row": twin}, device_id_type=MESH)
    for bit in order[0]:
        pl.semaphore_signal(barrier, inc=1, device_id={"col": flip(col, bit)}, device_id_type=MESH)

    @pl.when(has_left)
    def _():
        pl.semaphore_signal(barrier, inc=1, device_id={"row": row - CORES}, device_id_type=MESH)

    @pl.when(has_right)
    def _():
        pl.semaphore_signal(barrier, inc=1, device_id={"row": row + CORES}, device_id_type=MESH)

    def mask_int(j):
        for k in range(ktiles):
            scale = int_occ[k, j].astype(jnp.float32)
            block = integ[k * TILE:(k + 1) * TILE, j * TILE:(j + 1) * TILE].astype(jnp.float32) * scale
            gath[row * tiles + j, k * TILE:(k + 1) * TILE, :] = block.astype(jnp.bfloat16)

    mask_int(0)
    pl.semaphore_wait(barrier, 1 + len(order[0]) + has_left.astype(jnp.int32) + has_right.astype(jnp.int32))

    def hop(tile, send, target):
        return pltpu.make_async_remote_copy(
            src_ref=gath.at[tile], dst_ref=gath.at[tile], send_sem=send.at[tile],
            recv_sem=recv.at[tile], device_id={"row": target}, device_id_type=MESH)

    for j in range(tiles):
        if j > 0:
            mask_int(j)
        mine = row * tiles + j

        @pl.when(has_right)
        def _():
            hop(mine, right_send, row + CORES).start()

        @pl.when(has_left)
        def _():
            hop(mine, left_send, row - CORES).start()

        hop(mine, twin_send, twin).start()

    for i in range(nrows // TILE):
        for k in range(ktiles):
            scale = amp_occ[i, k].astype(jnp.float32)
            block = amp[i * TILE:(i + 1) * TILE, k * TILE:(k + 1) * TILE].astype(jnp.float32) * scale
            masked[i * TILE:(i + 1) * TILE, k * TILE:(k + 1) * TILE] = block.astype(jnp.bfloat16)

    for step in range(1, nz):
        for j in range(tiles):
            from_left = ((z - step) * CORES + core) * tiles + j
            from_right = ((z + step) * CORES + core) * tiles + j

            @pl.when(z >= step)
            def _():
                hop(from_left, right_send, twin).wait_recv()

                @pl.when(has_right)
                def _():
                    hop(from_left, right_send, row + CORES).start()

                hop(from_left, twin_send, twin).start()

            @pl.when(z + step < nz)
            def _():
                hop(from_right, left_send, twin).wait_recv()

                @pl.when(has_left)
                def _():
                    hop(from_right, left_send, row - CORES).start()

                hop(from_right, twin_send, twin).start()

    for other in range(nz):
        for j in range(tiles):
            hop((other * CORES + (CORES - 1) - core) * tiles + j, twin_send, twin).wait_recv()

    pair = 2 if per_col % 2 == 0 else 1

    def multiply(offset):
        base = flip(col, offset) * per_col

        @pl.loop(0, per_col // pair)
        def _(i):
            right = [gath[owner[base + i * pair + p]] for p in range(pair)]
            right = right[0] if pair == 1 else jnp.concatenate(right, axis=1)
            value = jnp.dot(masked[...], right, preferred_element_type=jnp.float32)
            at = pl.multiple_of(i * pair * TILE, pair * TILE)
            part[offset, :, pl.ds(at, pair * TILE)] = value.astype(jnp.bfloat16)

    slot = {}
    for h in range(2):
        for stage in range(len(order[h])):
            for offset in range(ncol):
                if not any(offset & bit for bit in order[h][:stage + 1]):
                    slot[h, stage, offset] = len(slot)

    def reduce_hop(h, offset):
        stage = first_stage(offset, order[h])
        bit = order[h][stage]
        there = slot[h, stage, offset ^ bit]
        return pltpu.make_async_remote_copy(
            src_ref=part.at[offset, pl.ds(h * half, half), :], dst_ref=landed.at[there],
            send_sem=col_send.at[there], recv_sem=col_recv.at[there],
            device_id={"col": flip(col, bit)}, device_id_type=MESH)

    def total(h, stages, offset):
        value = part[offset, h * half:(h + 1) * half, :].astype(jnp.float32)
        for stage in range(stages):
            value += landed[slot[h, stage, offset]].astype(jnp.float32)
        return value.astype(jnp.bfloat16)

    def arrived(h, stage, offset):
        reduce_hop(h, offset ^ order[h][stage]).wait_recv()

    for offset in range(ncol - 1, -1, -1):
        multiply(offset)
        for h in range(2):
            if first_stage(offset, order[h]) == 0:
                reduce_hop(h, offset).start()
    for stage in range(1, len(order[0])):
        for h in range(2):
            for offset in range(ncol - 1, 0, -1):
                if first_stage(offset, order[h]) == stage:
                    for before in range(stage):
                        arrived(h, before, offset)
                    part[offset, h * half:(h + 1) * half, :] = total(h, stage, offset)
                    reduce_hop(h, offset).start()
    for h in range(2):
        for stage in range(len(order[h])):
            arrived(h, stage, 0)
        out[h * half:(h + 1) * half, :] = total(h, len(order[h]), 0)

    for h in range(2):
        for offset in range(1, ncol):
            reduce_hop(h, offset).wait_send()
    for other in range(nz):
        for j in range(tiles):
            tile = (other * CORES + core) * tiles + j
            hop(tile, twin_send, twin).wait_send()

            @pl.when(has_right & (other <= z))
            def _():
                hop(tile, right_send, twin).wait_send()

            @pl.when(has_left & (other >= z))
            def _():
                hop(tile, left_send, twin).wait_send()


def on_device(nrow, ncol, amplitudes, integrals, amp_occupancy, int_occupancy, owner_map):
    rows, depth = amplitudes.shape
    tiles_all = nrow * integrals.shape[1] // TILE
    width = tiles_all * TILE // ncol
    vmem = pl.BlockSpec(memory_space=pltpu.VMEM)
    smem = pl.BlockSpec(memory_space=pltpu.SMEM)
    slots = 2 * (ncol - 1)
    return pl.pallas_call(
        functools.partial(kernel, nrow, ncol),
        out_shape=jax.ShapeDtypeStruct((rows, width), jnp.bfloat16),
        in_specs=[smem, smem, smem, vmem, vmem],
        out_specs=vmem,
        scratch_shapes=[
            pltpu.VMEM((rows, depth), jnp.bfloat16),
            pltpu.VMEM((tiles_all, depth, TILE), jnp.bfloat16),
            pltpu.VMEM((ncol, rows, width), jnp.bfloat16),
            pltpu.VMEM((slots, rows // 2, width), jnp.bfloat16),
            pltpu.SemaphoreType.DMA((tiles_all,)),
            pltpu.SemaphoreType.DMA((tiles_all,)),
            pltpu.SemaphoreType.DMA((tiles_all,)),
            pltpu.SemaphoreType.DMA((tiles_all,)),
            pltpu.SemaphoreType.DMA((slots,)),
            pltpu.SemaphoreType.DMA((slots,)),
        ],
        compiler_params=pltpu.CompilerParams(
            collective_id=0, has_side_effects=True, vmem_limit_bytes=48 * 1024 * 1024),
        cost_estimate=pl.CostEstimate(
            flops=2 * rows * depth * tiles_all * TILE, bytes_accessed=4 * rows * depth * 2, transcendentals=0),
    )(amp_occupancy, int_occupancy, owner_map, amplitudes, integrals)


def solution(mesh):
    placed = (P("row", "col"), P("col", "row"), P("row", "col"), P("col", "row"), P())
    body = functools.partial(on_device, mesh.shape["row"], mesh.shape["col"])
    return jax.shard_map(body, mesh=mesh, in_specs=placed, out_specs=P("row", "col"), check_vma=False)
```

```python
import functools

import jax
import jax.numpy as jnp
from jax import lax
from jax.experimental import pallas as pl
from jax.experimental.pallas import tpu as pltpu
from jax.sharding import PartitionSpec as P

TILE = 128
CORES = 2
LAG = 2
MESH = pl.DeviceIdType.MESH


def flip(value, mask):
    bit, out = 1, value
    while bit <= mask:
        if mask & bit:
            out = out + bit - 2 * bit * (lax.rem(value // bit, 2))
        bit *= 2
    return out


def orders(ncol):
    bits = [1 << i for i in range(ncol.bit_length() - 1)]
    return (bits, bits[::-1])


def kernel(nrow, ncol, amp_occ, int_occ, owner, amp, integ, out,
           masked, gath, part, landed, full, recv, right_send, left_send, twin_send,
           down_send, down_recv, up_send, up_recv):
    nz = nrow // CORES
    row, col = lax.axis_index("row"), lax.axis_index("col")
    z, core = row // CORES, lax.rem(row, CORES)
    twin = z * CORES + (CORES - 1) - core
    has_left, has_right = z > 0, z < nz - 1
    tiles = integ.shape[1] // TILE
    ktiles = integ.shape[0] // TILE
    nrows = amp.shape[0]
    width = out.shape[1]
    per_col = width // TILE
    order = orders(ncol)

    barrier = pltpu.get_barrier_semaphore()
    pl.semaphore_signal(barrier, inc=1, device_id={"row": twin}, device_id_type=MESH)
    for bit in order[0]:
        pl.semaphore_signal(barrier, inc=1, device_id={"col": flip(col, bit)}, device_id_type=MESH)

    @pl.when(has_left)
    def _():
        pl.semaphore_signal(barrier, inc=1, device_id={"row": row - CORES}, device_id_type=MESH)

    @pl.when(has_right)
    def _():
        pl.semaphore_signal(barrier, inc=1, device_id={"row": row + CORES}, device_id_type=MESH)

    def mask_int(j):
        for k in range(ktiles):
            scale = int_occ[k, j].astype(jnp.float32)
            block = integ[k * TILE:(k + 1) * TILE, j * TILE:(j + 1) * TILE].astype(jnp.float32) * scale
            gath[row * tiles + j, k * TILE:(k + 1) * TILE, :] = block.astype(jnp.bfloat16)

    mask_int(0)
    pl.semaphore_wait(barrier, 1 + len(order[0]) + has_left.astype(jnp.int32) + has_right.astype(jnp.int32))

    def hop(tile, send, target):
        return pltpu.make_async_remote_copy(
            src_ref=gath.at[tile], dst_ref=gath.at[tile], send_sem=send.at[tile],
            recv_sem=recv.at[tile], device_id={"row": target}, device_id_type=MESH)

    for j in range(tiles):
        if j > 0:
            mask_int(j)
        mine = row * tiles + j

        @pl.when(has_right)
        def _():
            hop(mine, right_send, row + CORES).start()

        @pl.when(has_left)
        def _():
            hop(mine, left_send, row - CORES).start()

        hop(mine, twin_send, twin).start()

    for i in range(nrows // TILE):
        for k in range(ktiles):
            scale = amp_occ[i, k].astype(jnp.float32)
            block = amp[i * TILE:(i + 1) * TILE, k * TILE:(k + 1) * TILE].astype(jnp.float32) * scale
            masked[i * TILE:(i + 1) * TILE, k * TILE:(k + 1) * TILE] = block.astype(jnp.bfloat16)

    levels = len(order[0])
    units = (nz - 1) * tiles

    def low(h, level):
        at = 0
        for k in range(level):
            at = at + lax.rem(col // order[h][k], 2) * (nrows >> (k + 1))
        return at

    def span(h, level):
        return pl.ds(pl.multiple_of(low(h, level), nrows >> level), nrows >> level)

    def slot(level):
        return pl.ds(nrows - (nrows >> level), nrows >> (level + 1))

    def down(h, level, tile):
        size = nrows >> (level + 1)
        start = low(h, level) + (1 - lax.rem(col // order[h][level], 2)) * size
        return pltpu.make_async_remote_copy(
            src_ref=part.at[tile, pl.ds(pl.multiple_of(start, size), size), :],
            dst_ref=landed.at[tile, slot(level), :],
            send_sem=down_send.at[tile, level], recv_sem=down_recv.at[tile, level],
            device_id={"col": flip(col, order[h][level])}, device_id_type=MESH)

    def up(h, level, tile):
        return pltpu.make_async_remote_copy(
            src_ref=full.at[tile, span(h, level + 1), :], dst_ref=full.at[tile, span(h, level + 1), :],
            send_sem=up_send.at[tile, level], recv_sem=up_recv.at[tile, level],
            device_id={"col": flip(col, order[h][level])}, device_id_type=MESH)

    def multiply(block, j):
        pair = [(block * CORES + c) * tiles + j for c in range(CORES)]
        hop((block * CORES + (CORES - 1) - core) * tiles + j, twin_send, twin).wait_recv()
        right = jnp.concatenate([gath[tile] for tile in pair], axis=1)
        value = jnp.dot(masked[...], right, preferred_element_type=jnp.float32).astype(jnp.bfloat16)
        for h, tile in enumerate(pair):
            part[tile] = value[:, h * TILE:(h + 1) * TILE]
            down(h, 0, tile).start()

    def advance(stage, block, j):
        for h in range(CORES):
            tile = (block * CORES + h) * tiles + j
            if stage < levels:
                down(h, stage, tile).wait_recv()
                keep = span(h, stage + 1)
                value = part[tile, keep, :].astype(jnp.float32) + landed[tile, slot(stage), :].astype(jnp.float32)
                if stage < levels - 1:
                    part[tile, keep, :] = value.astype(jnp.bfloat16)
                    down(h, stage + 1, tile).start()
                else:
                    full[tile, keep, :] = value.astype(jnp.bfloat16)
                    up(h, stage, tile).start()
            else:
                level = 2 * levels - 1 - stage
                up(h, level, tile).wait_recv()
                if level > 0:
                    up(h, level - 1, tile).start()

    def sides(n, lag, action):
        at = n - lag
        step, j = 1 + at // tiles, lax.rem(at, tiles)
        inside = (at >= 0) & (at < units)

        @pl.when((at >= 0) & (at < tiles))
        def _():
            action(z, at)

        @pl.when(inside & (z - step >= 0))
        def _():
            action(z - step, j)

        @pl.when(inside & (z + step < nz))
        def _():
            action(z + step, j)

    def forward(n):
        step, j = 1 + n // tiles, lax.rem(n, tiles)
        from_left = ((z - step) * CORES + core) * tiles + j
        from_right = ((z + step) * CORES + core) * tiles + j

        @pl.when((n < units) & (z - step >= 0))
        def _():
            hop(from_left, right_send, twin).wait_recv()

            @pl.when(has_right)
            def _():
                hop(from_left, right_send, row + CORES).start()

            hop(from_left, twin_send, twin).start()

        @pl.when((n < units) & (z + step < nz))
        def _():
            hop(from_right, left_send, twin).wait_recv()

            @pl.when(has_left)
            def _():
                hop(from_right, left_send, row - CORES).start()

            hop(from_right, twin_send, twin).start()

    @pl.loop(0, units + LAG * 2 * levels + 1)
    def _(n):
        forward(n)
        sides(n, 0, multiply)
        for stage in range(2 * levels):
            sides(n, LAG * (stage + 1), functools.partial(advance, stage))

    for t in range(per_col):
        out[:, t * TILE:(t + 1) * TILE] = full[owner[col * per_col + t]]

    @pl.loop(0, nz * tiles)
    def _(n):
        other, j = n // tiles, lax.rem(n, tiles)
        for h in range(CORES):
            tile = (other * CORES + h) * tiles + j
            for level in range(levels):
                down(h, level, tile).wait_send()
                up(h, level, tile).wait_send()
        mine = (other * CORES + core) * tiles + j
        hop(mine, twin_send, twin).wait_send()

        @pl.when(has_right & (other <= z))
        def _():
            hop(mine, right_send, twin).wait_send()

        @pl.when(has_left & (other >= z))
        def _():
            hop(mine, left_send, twin).wait_send()


def on_device(nrow, ncol, amplitudes, integrals, amp_occupancy, int_occupancy, owner_map):
    rows, depth = amplitudes.shape
    tiles_all = nrow * integrals.shape[1] // TILE
    width = tiles_all * TILE // ncol
    vmem = pl.BlockSpec(memory_space=pltpu.VMEM)
    smem = pl.BlockSpec(memory_space=pltpu.SMEM)
    levels = ncol.bit_length() - 1
    return pl.pallas_call(
        functools.partial(kernel, nrow, ncol),
        out_shape=jax.ShapeDtypeStruct((rows, width), jnp.bfloat16),
        in_specs=[smem, smem, smem, vmem, vmem],
        out_specs=vmem,
        scratch_shapes=[
            pltpu.VMEM((rows, depth), jnp.bfloat16),
            pltpu.VMEM((tiles_all, depth, TILE), jnp.bfloat16),
            pltpu.VMEM((tiles_all, rows, TILE), jnp.bfloat16),
            pltpu.VMEM((tiles_all, rows, TILE), jnp.bfloat16),
            pltpu.VMEM((tiles_all, rows, TILE), jnp.bfloat16),
            pltpu.SemaphoreType.DMA((tiles_all,)),
            pltpu.SemaphoreType.DMA((tiles_all,)),
            pltpu.SemaphoreType.DMA((tiles_all,)),
            pltpu.SemaphoreType.DMA((tiles_all,)),
            pltpu.SemaphoreType.DMA((tiles_all, levels)),
            pltpu.SemaphoreType.DMA((tiles_all, levels)),
            pltpu.SemaphoreType.DMA((tiles_all, levels)),
            pltpu.SemaphoreType.DMA((tiles_all, levels)),
        ],
        compiler_params=pltpu.CompilerParams(
            collective_id=0, has_side_effects=True, vmem_limit_bytes=48 * 1024 * 1024),
        cost_estimate=pl.CostEstimate(
            flops=2 * rows * depth * tiles_all * TILE, bytes_accessed=4 * rows * depth * 2, transcendentals=0),
    )(amp_occupancy, int_occupancy, owner_map, amplitudes, integrals)


def solution(mesh):
    placed = (P("row", "col"), P("col", "row"), P("row", "col"), P("col", "row"), P())
    body = functools.partial(on_device, mesh.shape["row"], mesh.shape["col"])
    return jax.shard_map(body, mesh=mesh, in_specs=placed, out_specs=P("row", "col"), check_vma=False)
```

```python
import functools

import jax
import jax.numpy as jnp
from jax import lax
from jax.experimental import pallas as pl
from jax.experimental.pallas import tpu as pltpu
from jax.sharding import PartitionSpec as P

TILE = 128
CORES = 2
END_LAG, INNER_LAG = 1, 3
MESH = pl.DeviceIdType.MESH


def flip(value, mask):
    bit, out = 1, value
    while bit <= mask:
        if mask & bit:
            out = out + bit - 2 * bit * (lax.rem(value // bit, 2))
        bit *= 2
    return out


def orders(ncol):
    bits = [1 << i for i in range(ncol.bit_length() - 1)]
    return (bits, bits[::-1])


def kernel(nrow, ncol, amp_occ, int_occ, owner, amp, integ, out,
           masked, gath, part, landed, full, recv, right_send, left_send, twin_send,
           down_send, down_recv, up_send, up_recv):
    nz = nrow // CORES
    row, col = lax.axis_index("row"), lax.axis_index("col")
    z, core = row // CORES, lax.rem(row, CORES)
    twin = z * CORES + (CORES - 1) - core
    has_left, has_right = z > 0, z < nz - 1
    tiles = integ.shape[1] // TILE
    ktiles = integ.shape[0] // TILE
    nrows = amp.shape[0]
    width = out.shape[1]
    per_col = width // TILE
    order = orders(ncol)

    barrier = pltpu.get_barrier_semaphore()
    pl.semaphore_signal(barrier, inc=1, device_id={"row": twin}, device_id_type=MESH)
    for bit in order[0]:
        pl.semaphore_signal(barrier, inc=1, device_id={"col": flip(col, bit)}, device_id_type=MESH)

    @pl.when(has_left)
    def _():
        pl.semaphore_signal(barrier, inc=1, device_id={"row": row - CORES}, device_id_type=MESH)

    @pl.when(has_right)
    def _():
        pl.semaphore_signal(barrier, inc=1, device_id={"row": row + CORES}, device_id_type=MESH)

    def mask_int(j):
        for k in range(ktiles):
            scale = int_occ[k, j].astype(jnp.float32)
            block = integ[k * TILE:(k + 1) * TILE, j * TILE:(j + 1) * TILE].astype(jnp.float32) * scale
            gath[row * tiles + j, k * TILE:(k + 1) * TILE, :] = block.astype(jnp.bfloat16)

    mask_int(0)
    pl.semaphore_wait(barrier, 1 + len(order[0]) + has_left.astype(jnp.int32) + has_right.astype(jnp.int32))

    def hop(tile, send, target):
        return pltpu.make_async_remote_copy(
            src_ref=gath.at[tile], dst_ref=gath.at[tile], send_sem=send.at[tile],
            recv_sem=recv.at[tile], device_id={"row": target}, device_id_type=MESH)

    for j in range(tiles):
        if j > 0:
            mask_int(j)
        mine = row * tiles + j

        @pl.when(has_right)
        def _():
            hop(mine, right_send, row + CORES).start()

        @pl.when(has_left)
        def _():
            hop(mine, left_send, row - CORES).start()

        hop(mine, twin_send, twin).start()

    for i in range(nrows // TILE):
        for k in range(ktiles):
            scale = amp_occ[i, k].astype(jnp.float32)
            block = amp[i * TILE:(i + 1) * TILE, k * TILE:(k + 1) * TILE].astype(jnp.float32) * scale
            masked[i * TILE:(i + 1) * TILE, k * TILE:(k + 1) * TILE] = block.astype(jnp.bfloat16)

    levels = len(order[0])
    units = (nz - 1) * tiles
    inner = has_left.astype(jnp.int32) * has_right.astype(jnp.int32)
    lag = END_LAG + (INNER_LAG - END_LAG) * inner

    def low(h, level):
        at = 0
        for k in range(level):
            at = at + lax.rem(col // order[h][k], 2) * (nrows >> (k + 1))
        return at

    def span(h, level):
        return pl.ds(pl.multiple_of(low(h, level), nrows >> level), nrows >> level)

    def slot(level):
        return pl.ds(nrows - (nrows >> level), nrows >> (level + 1))

    def down(h, level, tile):
        size = nrows >> (level + 1)
        start = low(h, level) + (1 - lax.rem(col // order[h][level], 2)) * size
        return pltpu.make_async_remote_copy(
            src_ref=part.at[tile, pl.ds(pl.multiple_of(start, size), size), :],
            dst_ref=landed.at[tile, slot(level), :],
            send_sem=down_send.at[tile, level], recv_sem=down_recv.at[tile, level],
            device_id={"col": flip(col, order[h][level])}, device_id_type=MESH)

    def up(h, level, tile):
        return pltpu.make_async_remote_copy(
            src_ref=full.at[tile, span(h, level + 1), :], dst_ref=full.at[tile, span(h, level + 1), :],
            send_sem=up_send.at[tile, level], recv_sem=up_recv.at[tile, level],
            device_id={"col": flip(col, order[h][level])}, device_id_type=MESH)

    def multiply(block, j):
        pair = [(block * CORES + c) * tiles + j for c in range(CORES)]
        hop((block * CORES + (CORES - 1) - core) * tiles + j, twin_send, twin).wait_recv()
        right = jnp.concatenate([gath[tile] for tile in pair], axis=1)
        value = jnp.dot(masked[...], right, preferred_element_type=jnp.float32).astype(jnp.bfloat16)
        for h, tile in enumerate(pair):
            part[tile] = value[:, h * TILE:(h + 1) * TILE]
            down(h, 0, tile).start()

    def advance(stage, block, j):
        for h in range(CORES):
            tile = (block * CORES + h) * tiles + j
            if stage < levels:
                down(h, stage, tile).wait_recv()
                keep = span(h, stage + 1)
                value = part[tile, keep, :].astype(jnp.float32) + landed[tile, slot(stage), :].astype(jnp.float32)
                if stage < levels - 1:
                    part[tile, keep, :] = value.astype(jnp.bfloat16)
                    down(h, stage + 1, tile).start()
                else:
                    full[tile, keep, :] = value.astype(jnp.bfloat16)
                    up(h, stage, tile).start()
            else:
                level = 2 * levels - 1 - stage
                up(h, level, tile).wait_recv()
                if level > 0:
                    up(h, level - 1, tile).start()

    def sides(n, behind, action):
        at = n - behind
        step, j = 1 + at // tiles, lax.rem(at, tiles)
        inside = (at >= 0) & (at < units)

        @pl.when((at >= 0) & (at < tiles))
        def _():
            action(z, at)

        @pl.when(inside & (z - step >= 0))
        def _():
            action(z - step, j)

        @pl.when(inside & (z + step < nz))
        def _():
            action(z + step, j)

    def forward(n):
        step, j = 1 + n // tiles, lax.rem(n, tiles)
        from_left = ((z - step) * CORES + core) * tiles + j
        from_right = ((z + step) * CORES + core) * tiles + j

        @pl.when((n < units) & (z - step >= 0))
        def _():
            hop(from_left, right_send, twin).wait_recv()

            @pl.when(has_right)
            def _():
                hop(from_left, right_send, row + CORES).start()

            hop(from_left, twin_send, twin).start()

        @pl.when((n < units) & (z + step < nz))
        def _():
            hop(from_right, left_send, twin).wait_recv()

            @pl.when(has_left)
            def _():
                hop(from_right, left_send, row - CORES).start()

            hop(from_right, twin_send, twin).start()

    @pl.loop(0, units + INNER_LAG * 2 * levels + 1)
    def _(n):
        forward(n)
        sides(n, 0, multiply)
        for stage in range(2 * levels):
            sides(n, lag * (stage + 1), functools.partial(advance, stage))

    for t in range(per_col):
        out[:, t * TILE:(t + 1) * TILE] = full[owner[col * per_col + t]]

    @pl.loop(0, nz * tiles)
    def _(n):
        other, j = n // tiles, lax.rem(n, tiles)
        for h in range(CORES):
            tile = (other * CORES + h) * tiles + j
            for level in range(levels):
                down(h, level, tile).wait_send()
                up(h, level, tile).wait_send()
        mine = (other * CORES + core) * tiles + j
        hop(mine, twin_send, twin).wait_send()

        @pl.when(has_right & (other <= z))
        def _():
            hop(mine, right_send, twin).wait_send()

        @pl.when(has_left & (other >= z))
        def _():
            hop(mine, left_send, twin).wait_send()


def on_device(nrow, ncol, amplitudes, integrals, amp_occupancy, int_occupancy, owner_map):
    rows, depth = amplitudes.shape
    tiles_all = nrow * integrals.shape[1] // TILE
    width = tiles_all * TILE // ncol
    vmem = pl.BlockSpec(memory_space=pltpu.VMEM)
    smem = pl.BlockSpec(memory_space=pltpu.SMEM)
    levels = ncol.bit_length() - 1
    return pl.pallas_call(
        functools.partial(kernel, nrow, ncol),
        out_shape=jax.ShapeDtypeStruct((rows, width), jnp.bfloat16),
        in_specs=[smem, smem, smem, vmem, vmem],
        out_specs=vmem,
        scratch_shapes=[
            pltpu.VMEM((rows, depth), jnp.bfloat16),
            pltpu.VMEM((tiles_all, depth, TILE), jnp.bfloat16),
            pltpu.VMEM((tiles_all, rows, TILE), jnp.bfloat16),
            pltpu.VMEM((tiles_all, rows, TILE), jnp.bfloat16),
            pltpu.VMEM((tiles_all, rows, TILE), jnp.bfloat16),
            pltpu.SemaphoreType.DMA((tiles_all,)),
            pltpu.SemaphoreType.DMA((tiles_all,)),
            pltpu.SemaphoreType.DMA((tiles_all,)),
            pltpu.SemaphoreType.DMA((tiles_all,)),
            pltpu.SemaphoreType.DMA((tiles_all, levels)),
            pltpu.SemaphoreType.DMA((tiles_all, levels)),
            pltpu.SemaphoreType.DMA((tiles_all, levels)),
            pltpu.SemaphoreType.DMA((tiles_all, levels)),
        ],
        compiler_params=pltpu.CompilerParams(
            collective_id=0, has_side_effects=True, vmem_limit_bytes=48 * 1024 * 1024),
        cost_estimate=pl.CostEstimate(
            flops=2 * rows * depth * tiles_all * TILE, bytes_accessed=4 * rows * depth * 2, transcendentals=0),
    )(amp_occupancy, int_occupancy, owner_map, amplitudes, integrals)


def solution(mesh):
    placed = (P("row", "col"), P("col", "row"), P("row", "col"), P("col", "row"), P())
    body = functools.partial(on_device, mesh.shape["row"], mesh.shape["col"])
    return jax.shard_map(body, mesh=mesh, in_specs=placed, out_specs=P("row", "col"), check_vma=False)
```

```python
import functools

import jax
import jax.numpy as jnp
from jax import lax
from jax.experimental import pallas as pl
from jax.experimental.pallas import tpu as pltpu
from jax.sharding import PartitionSpec as P

TILE = 128
CORES = 2
END_LAG, INNER_LAG = 1, 2
MESH = pl.DeviceIdType.MESH


def flip(value, mask):
    bit, out = 1, value
    while bit <= mask:
        if mask & bit:
            out = out + bit - 2 * bit * (lax.rem(value // bit, 2))
        bit *= 2
    return out


def orders(ncol):
    bits = [1 << i for i in range(ncol.bit_length() - 1)]
    return (bits, bits[::-1])


def early_rows(rows, ncol):
    unit = 16 * ncol
    return max(unit, rows * 3 // 4 // unit * unit)


def first_stage(offset, order):
    return next(i for i, bit in enumerate(order) if offset & bit)


def kernel(nrow, ncol, amp_occ, int_occ, owner, amp, integ, out,
           masked, gath, part, landed, full, recv, right_send, left_send, twin_send,
           down_send, down_recv, up_send, up_recv,
           late, late_landed, late_send, late_recv):
    nz = nrow // CORES
    row, col = lax.axis_index("row"), lax.axis_index("col")
    z, core = row // CORES, lax.rem(row, CORES)
    twin = z * CORES + (CORES - 1) - core
    has_left, has_right = z > 0, z < nz - 1
    tiles = integ.shape[1] // TILE
    ktiles = integ.shape[0] // TILE
    nrows = amp.shape[0]
    width = out.shape[1]
    per_col = width // TILE
    order = orders(ncol)

    barrier = pltpu.get_barrier_semaphore()
    pl.semaphore_signal(barrier, inc=1, device_id={"row": twin}, device_id_type=MESH)
    for bit in order[0]:
        pl.semaphore_signal(barrier, inc=1, device_id={"col": flip(col, bit)}, device_id_type=MESH)

    @pl.when(has_left)
    def _():
        pl.semaphore_signal(barrier, inc=1, device_id={"row": row - CORES}, device_id_type=MESH)

    @pl.when(has_right)
    def _():
        pl.semaphore_signal(barrier, inc=1, device_id={"row": row + CORES}, device_id_type=MESH)

    def mask_int(j):
        for k in range(ktiles):
            scale = int_occ[k, j].astype(jnp.float32)
            block = integ[k * TILE:(k + 1) * TILE, j * TILE:(j + 1) * TILE].astype(jnp.float32) * scale
            gath[row * tiles + j, k * TILE:(k + 1) * TILE, :] = block.astype(jnp.bfloat16)

    mask_int(0)
    pl.semaphore_wait(barrier, 1 + len(order[0]) + has_left.astype(jnp.int32) + has_right.astype(jnp.int32))

    def hop(tile, send, target):
        return pltpu.make_async_remote_copy(
            src_ref=gath.at[tile], dst_ref=gath.at[tile], send_sem=send.at[tile],
            recv_sem=recv.at[tile], device_id={"row": target}, device_id_type=MESH)

    for j in range(tiles):
        if j > 0:
            mask_int(j)
        mine = row * tiles + j

        @pl.when(has_right)
        def _():
            hop(mine, right_send, row + CORES).start()

        @pl.when(has_left)
        def _():
            hop(mine, left_send, row - CORES).start()

        hop(mine, twin_send, twin).start()

    for i in range(nrows // TILE):
        for k in range(ktiles):
            scale = amp_occ[i, k].astype(jnp.float32)
            block = amp[i * TILE:(i + 1) * TILE, k * TILE:(k + 1) * TILE].astype(jnp.float32) * scale
            masked[i * TILE:(i + 1) * TILE, k * TILE:(k + 1) * TILE] = block.astype(jnp.bfloat16)

    levels = len(order[0])
    early = part.shape[1]
    half = (nrows - early) // 2
    units = (nz - 1) * tiles
    inner = has_left.astype(jnp.int32) * has_right.astype(jnp.int32)
    lag = END_LAG + (INNER_LAG - END_LAG) * inner

    def low(h, level):
        at = 0
        for k in range(level):
            at = at + lax.rem(col // order[h][k], 2) * (early >> (k + 1))
        return at

    def span(h, level):
        return pl.ds(pl.multiple_of(low(h, level), early >> level), early >> level)

    def slot(level):
        return pl.ds(early - (early >> level), early >> (level + 1))

    def down(h, level, tile):
        size = early >> (level + 1)
        start = low(h, level) + (1 - lax.rem(col // order[h][level], 2)) * size
        return pltpu.make_async_remote_copy(
            src_ref=part.at[tile, pl.ds(pl.multiple_of(start, size), size), :],
            dst_ref=landed.at[tile, slot(level), :],
            send_sem=down_send.at[tile, level], recv_sem=down_recv.at[tile, level],
            device_id={"col": flip(col, order[h][level])}, device_id_type=MESH)

    def up(h, level, tile):
        return pltpu.make_async_remote_copy(
            src_ref=full.at[tile, span(h, level + 1), :], dst_ref=full.at[tile, span(h, level + 1), :],
            send_sem=up_send.at[tile, level], recv_sem=up_recv.at[tile, level],
            device_id={"col": flip(col, order[h][level])}, device_id_type=MESH)

    def multiply(block, j):
        pair = [(block * CORES + c) * tiles + j for c in range(CORES)]
        hop((block * CORES + (CORES - 1) - core) * tiles + j, twin_send, twin).wait_recv()
        right = jnp.concatenate([gath[tile] for tile in pair], axis=1)
        value = jnp.dot(masked[:early, :], right, preferred_element_type=jnp.float32).astype(jnp.bfloat16)
        for h, tile in enumerate(pair):
            part[tile] = value[:, h * TILE:(h + 1) * TILE]
            down(h, 0, tile).start()

    def advance(stage, block, j):
        for h in range(CORES):
            tile = (block * CORES + h) * tiles + j
            if stage < levels:
                down(h, stage, tile).wait_recv()
                keep = span(h, stage + 1)
                value = part[tile, keep, :].astype(jnp.float32) + landed[tile, slot(stage), :].astype(jnp.float32)
                if stage < levels - 1:
                    part[tile, keep, :] = value.astype(jnp.bfloat16)
                    down(h, stage + 1, tile).start()
                else:
                    full[tile, keep, :] = value.astype(jnp.bfloat16)
                    up(h, stage, tile).start()
            else:
                level = 2 * levels - 1 - stage
                up(h, level, tile).wait_recv()
                if level > 0:
                    up(h, level - 1, tile).start()

    def sides(n, behind, action):
        at = n - behind
        step, j = 1 + at // tiles, lax.rem(at, tiles)
        inside = (at >= 0) & (at < units)

        @pl.when((at >= 0) & (at < tiles))
        def _():
            action(z, at)

        @pl.when(inside & (z - step >= 0))
        def _():
            action(z - step, j)

        @pl.when(inside & (z + step < nz))
        def _():
            action(z + step, j)

    def forward(n):
        step, j = 1 + n // tiles, lax.rem(n, tiles)
        from_left = ((z - step) * CORES + core) * tiles + j
        from_right = ((z + step) * CORES + core) * tiles + j

        @pl.when((n < units) & (z - step >= 0))
        def _():
            hop(from_left, right_send, twin).wait_recv()

            @pl.when(has_right)
            def _():
                hop(from_left, right_send, row + CORES).start()

            hop(from_left, twin_send, twin).start()

        @pl.when((n < units) & (z + step < nz))
        def _():
            hop(from_right, left_send, twin).wait_recv()

            @pl.when(has_left)
            def _():
                hop(from_right, left_send, row - CORES).start()

            hop(from_right, twin_send, twin).start()

    group = 2 if per_col % 2 == 0 else 1

    def multiply_late(offset):
        base = flip(col, offset) * per_col

        @pl.loop(0, per_col // group)
        def _(i):
            right = [gath[owner[base + i * group + p]] for p in range(group)]
            right = right[0] if group == 1 else jnp.concatenate(right, axis=1)
            value = jnp.dot(masked[early:, :], right, preferred_element_type=jnp.float32)
            at = pl.multiple_of(i * group * TILE, group * TILE)
            late[offset, :, pl.ds(at, group * TILE)] = value.astype(jnp.bfloat16)

    place = {}
    for h in range(2):
        for stage in range(levels):
            for offset in range(ncol):
                if not any(offset & bit for bit in order[h][:stage + 1]):
                    place[h, stage, offset] = len(place)

    def late_hop(h, offset):
        stage = first_stage(offset, order[h])
        bit = order[h][stage]
        there = place[h, stage, offset ^ bit]
        return pltpu.make_async_remote_copy(
            src_ref=late.at[offset, pl.ds(h * half, half), :], dst_ref=late_landed.at[there],
            send_sem=late_send.at[there], recv_sem=late_recv.at[there],
            device_id={"col": flip(col, bit)}, device_id_type=MESH)

    def late_total(h, stages, offset):
        value = late[offset, h * half:(h + 1) * half, :].astype(jnp.float32)
        for stage in range(stages):
            late_hop(h, offset ^ order[h][stage]).wait_recv()
            value += late_landed[place[h, stage, offset]].astype(jnp.float32)
        return value.astype(jnp.bfloat16)

    @pl.loop(0, units)
    def _(n):
        forward(n)
        sides(n, 0, multiply)
        for stage in range(2 * levels):
            sides(n, lag * (stage + 1), functools.partial(advance, stage))

    for offset in range(ncol - 1, -1, -1):
        multiply_late(offset)
        for h in range(2):
            if offset and first_stage(offset, order[h]) == 0:
                late_hop(h, offset).start()

    @pl.loop(units, units + INNER_LAG * 2 * levels + 1)
    def _(n):
        for stage in range(2 * levels):
            sides(n, lag * (stage + 1), functools.partial(advance, stage))

    for stage in range(1, levels):
        for h in range(2):
            for offset in range(ncol - 1, 0, -1):
                if first_stage(offset, order[h]) == stage:
                    late[offset, h * half:(h + 1) * half, :] = late_total(h, stage, offset)
                    late_hop(h, offset).start()
    for t in range(per_col):
        out[:early, t * TILE:(t + 1) * TILE] = full[owner[col * per_col + t]]
    for h in range(2):
        out[early + h * half:early + (h + 1) * half, :] = late_total(h, levels, 0)
        for offset in range(1, ncol):
            late_hop(h, offset).wait_send()

    @pl.loop(0, nz * tiles)
    def _(n):
        other, j = n // tiles, lax.rem(n, tiles)
        for h in range(CORES):
            tile = (other * CORES + h) * tiles + j
            for level in range(levels):
                down(h, level, tile).wait_send()
                up(h, level, tile).wait_send()
        mine = (other * CORES + core) * tiles + j
        hop(mine, twin_send, twin).wait_send()

        @pl.when(has_right & (other <= z))
        def _():
            hop(mine, right_send, twin).wait_send()

        @pl.when(has_left & (other >= z))
        def _():
            hop(mine, left_send, twin).wait_send()


def on_device(nrow, ncol, amplitudes, integrals, amp_occupancy, int_occupancy, owner_map):
    rows, depth = amplitudes.shape
    tiles_all = nrow * integrals.shape[1] // TILE
    width = tiles_all * TILE // ncol
    early = early_rows(rows, ncol)
    places = 2 * (ncol - 1)
    vmem = pl.BlockSpec(memory_space=pltpu.VMEM)
    smem = pl.BlockSpec(memory_space=pltpu.SMEM)
    levels = ncol.bit_length() - 1
    return pl.pallas_call(
        functools.partial(kernel, nrow, ncol),
        out_shape=jax.ShapeDtypeStruct((rows, width), jnp.bfloat16),
        in_specs=[smem, smem, smem, vmem, vmem],
        out_specs=vmem,
        scratch_shapes=[
            pltpu.VMEM((rows, depth), jnp.bfloat16),
            pltpu.VMEM((tiles_all, depth, TILE), jnp.bfloat16),
            pltpu.VMEM((tiles_all, early, TILE), jnp.bfloat16),
            pltpu.VMEM((tiles_all, early, TILE), jnp.bfloat16),
            pltpu.VMEM((tiles_all, early, TILE), jnp.bfloat16),
            pltpu.SemaphoreType.DMA((tiles_all,)),
            pltpu.SemaphoreType.DMA((tiles_all,)),
            pltpu.SemaphoreType.DMA((tiles_all,)),
            pltpu.SemaphoreType.DMA((tiles_all,)),
            pltpu.SemaphoreType.DMA((tiles_all, levels)),
            pltpu.SemaphoreType.DMA((tiles_all, levels)),
            pltpu.SemaphoreType.DMA((tiles_all, levels)),
            pltpu.SemaphoreType.DMA((tiles_all, levels)),
            pltpu.VMEM((ncol, rows - early, width), jnp.bfloat16),
            pltpu.VMEM((places, (rows - early) // 2, width), jnp.bfloat16),
            pltpu.SemaphoreType.DMA((places,)),
            pltpu.SemaphoreType.DMA((places,)),
        ],
        compiler_params=pltpu.CompilerParams(
            collective_id=0, has_side_effects=True, vmem_limit_bytes=48 * 1024 * 1024),
        cost_estimate=pl.CostEstimate(
            flops=2 * rows * depth * tiles_all * TILE, bytes_accessed=4 * rows * depth * 2, transcendentals=0),
    )(amp_occupancy, int_occupancy, owner_map, amplitudes, integrals)


def solution(mesh):
    placed = (P("row", "col"), P("col", "row"), P("row", "col"), P("col", "row"), P())
    body = functools.partial(on_device, mesh.shape["row"], mesh.shape["col"])
    return jax.shard_map(body, mesh=mesh, in_specs=placed, out_specs=P("row", "col"), check_vma=False)
```

```python
import functools

import jax
import jax.numpy as jnp
from jax import lax
from jax.experimental import pallas as pl
from jax.experimental.pallas import tpu as pltpu
from jax.sharding import PartitionSpec as P

TILE = 128
CORES = 2
END_LAG, INNER_LAG = 1, 2
MESH = pl.DeviceIdType.MESH


def flip(value, mask):
    bit, out = 1, value
    while bit <= mask:
        if mask & bit:
            out = out + bit - 2 * bit * (lax.rem(value // bit, 2))
        bit *= 2
    return out


def orders(ncol):
    bits = [1 << i for i in range(ncol.bit_length() - 1)]
    return (bits, bits[::-1])


def kernel(nrow, ncol, amp_occ, int_occ, owner, amp, integ, out,
           masked, gath, part, landed, full, recv, right_send, left_send, twin_send,
           down_send, down_recv, up_send, up_recv):
    nz = nrow // CORES
    row, col = lax.axis_index("row"), lax.axis_index("col")
    z, core = row // CORES, lax.rem(row, CORES)
    twin = z * CORES + (CORES - 1) - core
    has_left, has_right = z > 0, z < nz - 1
    tiles = integ.shape[1] // TILE
    ktiles = integ.shape[0] // TILE
    nrows = amp.shape[0]
    width = out.shape[1]
    per_col = width // TILE
    order = orders(ncol)

    barrier = pltpu.get_barrier_semaphore()
    pl.semaphore_signal(barrier, inc=1, device_id={"row": twin}, device_id_type=MESH)
    for bit in order[0]:
        pl.semaphore_signal(barrier, inc=1, device_id={"col": flip(col, bit)}, device_id_type=MESH)

    @pl.when(has_left)
    def _():
        pl.semaphore_signal(barrier, inc=1, device_id={"row": row - CORES}, device_id_type=MESH)

    @pl.when(has_right)
    def _():
        pl.semaphore_signal(barrier, inc=1, device_id={"row": row + CORES}, device_id_type=MESH)

    def mask_int(j):
        for k in range(ktiles):
            scale = int_occ[k, j].astype(jnp.float32)
            block = integ[k * TILE:(k + 1) * TILE, j * TILE:(j + 1) * TILE].astype(jnp.float32) * scale
            gath[row * tiles + j, k * TILE:(k + 1) * TILE, :] = block.astype(jnp.bfloat16)

    mask_int(0)
    pl.semaphore_wait(barrier, 1 + len(order[0]) + has_left.astype(jnp.int32) + has_right.astype(jnp.int32))

    def hop(tile, send, target):
        return pltpu.make_async_remote_copy(
            src_ref=gath.at[tile], dst_ref=gath.at[tile], send_sem=send.at[tile],
            recv_sem=recv.at[tile], device_id={"row": target}, device_id_type=MESH)

    for j in range(tiles):
        if j > 0:
            mask_int(j)
        mine = row * tiles + j

        @pl.when(has_right)
        def _():
            hop(mine, right_send, row + CORES).start()

        @pl.when(has_left)
        def _():
            hop(mine, left_send, row - CORES).start()

        hop(mine, twin_send, twin).start()

    for i in range(nrows // TILE):
        for k in range(ktiles):
            scale = amp_occ[i, k].astype(jnp.float32)
            block = amp[i * TILE:(i + 1) * TILE, k * TILE:(k + 1) * TILE].astype(jnp.float32) * scale
            masked[i * TILE:(i + 1) * TILE, k * TILE:(k + 1) * TILE] = block.astype(jnp.bfloat16)

    levels = len(order[0])
    units = (nz - 1) * tiles
    inner = has_left.astype(jnp.int32) * has_right.astype(jnp.int32)
    lag = END_LAG + (INNER_LAG - END_LAG) * inner

    def low(h, level):
        at = 0
        for k in range(level):
            at = at + lax.rem(col // order[h][k], 2) * (nrows >> (k + 1))
        return at

    def span(h, level):
        return pl.ds(pl.multiple_of(low(h, level), nrows >> level), nrows >> level)

    def slot(level):
        return pl.ds(nrows - (nrows >> level), nrows >> (level + 1))

    def down(h, level, tile):
        size = nrows >> (level + 1)
        start = low(h, level) + (1 - lax.rem(col // order[h][level], 2)) * size
        return pltpu.make_async_remote_copy(
            src_ref=part.at[tile, pl.ds(pl.multiple_of(start, size), size), :],
            dst_ref=landed.at[tile, slot(level), :],
            send_sem=down_send.at[tile, level], recv_sem=down_recv.at[tile, level],
            device_id={"col": flip(col, order[h][level])}, device_id_type=MESH)

    def up(h, level, tile):
        return pltpu.make_async_remote_copy(
            src_ref=full.at[tile, span(h, level + 1), :], dst_ref=full.at[tile, span(h, level + 1), :],
            send_sem=up_send.at[tile, level], recv_sem=up_recv.at[tile, level],
            device_id={"col": flip(col, order[h][level])}, device_id_type=MESH)

    def multiply(block, j):
        pair = [(block * CORES + c) * tiles + j for c in range(CORES)]
        hop((block * CORES + (CORES - 1) - core) * tiles + j, twin_send, twin).wait_recv()
        right = jnp.concatenate([gath[tile] for tile in pair], axis=1)
        value = jnp.dot(masked[...], right, preferred_element_type=jnp.float32).astype(jnp.bfloat16)
        for h, tile in enumerate(pair):
            part[tile] = value[:, h * TILE:(h + 1) * TILE]
            down(h, 0, tile).start()

    def advance(stage, block, j):
        for h in range(CORES):
            tile = (block * CORES + h) * tiles + j
            if stage < levels:
                down(h, stage, tile).wait_recv()
                keep = span(h, stage + 1)
                value = part[tile, keep, :].astype(jnp.float32) + landed[tile, slot(stage), :].astype(jnp.float32)
                if stage < levels - 1:
                    part[tile, keep, :] = value.astype(jnp.bfloat16)
                    down(h, stage + 1, tile).start()
                else:
                    full[tile, keep, :] = value.astype(jnp.bfloat16)
                    up(h, stage, tile).start()
            else:
                level = 2 * levels - 1 - stage
                up(h, level, tile).wait_recv()
                if level > 0:
                    up(h, level - 1, tile).start()

    def sides(n, behind, action):
        at = n - behind
        step, j = 1 + at // tiles, lax.rem(at, tiles)
        inside = (at >= 0) & (at < units)

        @pl.when((at >= 0) & (at < 2 * tiles) & (lax.rem(at, 2) == 0))
        def _():
            action(z, at // 2)

        @pl.when(inside & (z - step >= 0))
        def _():
            action(z - step, j)

        @pl.when(inside & (z + step < nz))
        def _():
            action(z + step, j)

    def forward(n):
        step, j = 1 + n // tiles, lax.rem(n, tiles)
        from_left = ((z - step) * CORES + core) * tiles + j
        from_right = ((z + step) * CORES + core) * tiles + j

        @pl.when((n < units) & (z - step >= 0))
        def _():
            hop(from_left, right_send, twin).wait_recv()

            @pl.when(has_right)
            def _():
                hop(from_left, right_send, row + CORES).start()

            hop(from_left, twin_send, twin).start()

        @pl.when((n < units) & (z + step < nz))
        def _():
            hop(from_right, left_send, twin).wait_recv()

            @pl.when(has_left)
            def _():
                hop(from_right, left_send, row - CORES).start()

            hop(from_right, twin_send, twin).start()

    @pl.loop(0, max(units, 2 * tiles) + INNER_LAG * 2 * levels + 1)
    def _(n):
        forward(n)
        sides(n, 0, multiply)
        for stage in range(2 * levels):
            sides(n, lag * (stage + 1), functools.partial(advance, stage))

    for t in range(per_col):
        out[:, t * TILE:(t + 1) * TILE] = full[owner[col * per_col + t]]

    @pl.loop(0, nz * tiles)
    def _(n):
        other, j = n // tiles, lax.rem(n, tiles)
        for h in range(CORES):
            tile = (other * CORES + h) * tiles + j
            for level in range(levels):
                down(h, level, tile).wait_send()
                up(h, level, tile).wait_send()
        mine = (other * CORES + core) * tiles + j
        hop(mine, twin_send, twin).wait_send()

        @pl.when(has_right & (other <= z))
        def _():
            hop(mine, right_send, twin).wait_send()

        @pl.when(has_left & (other >= z))
        def _():
            hop(mine, left_send, twin).wait_send()


def on_device(nrow, ncol, amplitudes, integrals, amp_occupancy, int_occupancy, owner_map):
    rows, depth = amplitudes.shape
    tiles_all = nrow * integrals.shape[1] // TILE
    width = tiles_all * TILE // ncol
    vmem = pl.BlockSpec(memory_space=pltpu.VMEM)
    smem = pl.BlockSpec(memory_space=pltpu.SMEM)
    levels = ncol.bit_length() - 1
    return pl.pallas_call(
        functools.partial(kernel, nrow, ncol),
        out_shape=jax.ShapeDtypeStruct((rows, width), jnp.bfloat16),
        in_specs=[smem, smem, smem, vmem, vmem],
        out_specs=vmem,
        scratch_shapes=[
            pltpu.VMEM((rows, depth), jnp.bfloat16),
            pltpu.VMEM((tiles_all, depth, TILE), jnp.bfloat16),
            pltpu.VMEM((tiles_all, rows, TILE), jnp.bfloat16),
            pltpu.VMEM((tiles_all, rows, TILE), jnp.bfloat16),
            pltpu.VMEM((tiles_all, rows, TILE), jnp.bfloat16),
            pltpu.SemaphoreType.DMA((tiles_all,)),
            pltpu.SemaphoreType.DMA((tiles_all,)),
            pltpu.SemaphoreType.DMA((tiles_all,)),
            pltpu.SemaphoreType.DMA((tiles_all,)),
            pltpu.SemaphoreType.DMA((tiles_all, levels)),
            pltpu.SemaphoreType.DMA((tiles_all, levels)),
            pltpu.SemaphoreType.DMA((tiles_all, levels)),
            pltpu.SemaphoreType.DMA((tiles_all, levels)),
        ],
        compiler_params=pltpu.CompilerParams(
            collective_id=0, has_side_effects=True, vmem_limit_bytes=48 * 1024 * 1024),
        cost_estimate=pl.CostEstimate(
            flops=2 * rows * depth * tiles_all * TILE, bytes_accessed=4 * rows * depth * 2, transcendentals=0),
    )(amp_occupancy, int_occupancy, owner_map, amplitudes, integrals)


def solution(mesh):
    placed = (P("row", "col"), P("col", "row"), P("row", "col"), P("col", "row"), P())
    body = functools.partial(on_device, mesh.shape["row"], mesh.shape["col"])
    return jax.shard_map(body, mesh=mesh, in_specs=placed, out_specs=P("row", "col"), check_vma=False)
```

```python
import functools

import jax
import jax.numpy as jnp
from jax import lax
from jax.experimental import pallas as pl
from jax.experimental.pallas import tpu as pltpu
from jax.sharding import PartitionSpec as P

TILE = 128
CORES = 2
INNER_LAG = 2
MESH = pl.DeviceIdType.MESH


def flip(value, mask):
    bit, out = 1, value
    while bit <= mask:
        if mask & bit:
            out = out + bit - 2 * bit * (lax.rem(value // bit, 2))
        bit *= 2
    return out


def orders(ncol):
    bits = [1 << i for i in range(ncol.bit_length() - 1)]
    return (bits, bits[::-1])


def kernel(nrow, ncol, amp_occ, int_occ, owner, amp, integ, out,
           masked, gath, part, landed, full, recv, right_send, left_send, twin_send,
           down_send, down_recv, up_send, up_recv):
    nz = nrow // CORES
    row, col = lax.axis_index("row"), lax.axis_index("col")
    z, core = row // CORES, lax.rem(row, CORES)
    twin = z * CORES + (CORES - 1) - core
    has_left, has_right = z > 0, z < nz - 1
    tiles = integ.shape[1] // TILE
    ktiles = integ.shape[0] // TILE
    nrows = amp.shape[0]
    width = out.shape[1]
    per_col = width // TILE
    order = orders(ncol)

    barrier = pltpu.get_barrier_semaphore()
    pl.semaphore_signal(barrier, inc=1, device_id={"row": twin}, device_id_type=MESH)
    for bit in order[0]:
        pl.semaphore_signal(barrier, inc=1, device_id={"col": flip(col, bit)}, device_id_type=MESH)

    @pl.when(has_left)
    def _():
        pl.semaphore_signal(barrier, inc=1, device_id={"row": row - CORES}, device_id_type=MESH)

    @pl.when(has_right)
    def _():
        pl.semaphore_signal(barrier, inc=1, device_id={"row": row + CORES}, device_id_type=MESH)

    def mask_int(j):
        for k in range(ktiles):
            scale = int_occ[k, j].astype(jnp.float32)
            block = integ[k * TILE:(k + 1) * TILE, j * TILE:(j + 1) * TILE].astype(jnp.float32) * scale
            gath[row * tiles + j, k * TILE:(k + 1) * TILE, :] = block.astype(jnp.bfloat16)

    mask_int(0)
    pl.semaphore_wait(barrier, 1 + len(order[0]) + has_left.astype(jnp.int32) + has_right.astype(jnp.int32))

    def hop(tile, send, target):
        return pltpu.make_async_remote_copy(
            src_ref=gath.at[tile], dst_ref=gath.at[tile], send_sem=send.at[tile],
            recv_sem=recv.at[tile], device_id={"row": target}, device_id_type=MESH)

    for j in range(tiles):
        if j > 0:
            mask_int(j)
        mine = row * tiles + j

        @pl.when(has_right)
        def _():
            hop(mine, right_send, row + CORES).start()

        @pl.when(has_left)
        def _():
            hop(mine, left_send, row - CORES).start()

        hop(mine, twin_send, twin).start()

    for i in range(nrows // TILE):
        for k in range(ktiles):
            scale = amp_occ[i, k].astype(jnp.float32)
            block = amp[i * TILE:(i + 1) * TILE, k * TILE:(k + 1) * TILE].astype(jnp.float32) * scale
            masked[i * TILE:(i + 1) * TILE, k * TILE:(k + 1) * TILE] = block.astype(jnp.bfloat16)

    levels = len(order[0])
    units = (nz - 1) * tiles
    inner = has_left.astype(jnp.int32) * has_right.astype(jnp.int32)

    def low(h, level):
        at = 0
        for k in range(level):
            at = at + lax.rem(col // order[h][k], 2) * (nrows >> (k + 1))
        return at

    def span(h, level):
        return pl.ds(pl.multiple_of(low(h, level), nrows >> level), nrows >> level)

    def slot(level):
        return pl.ds(nrows - (nrows >> level), nrows >> (level + 1))

    def down(h, level, tile):
        size = nrows >> (level + 1)
        start = low(h, level) + (1 - lax.rem(col // order[h][level], 2)) * size
        return pltpu.make_async_remote_copy(
            src_ref=part.at[tile, pl.ds(pl.multiple_of(start, size), size), :],
            dst_ref=landed.at[tile, slot(level), :],
            send_sem=down_send.at[tile, level], recv_sem=down_recv.at[tile, level],
            device_id={"col": flip(col, order[h][level])}, device_id_type=MESH)

    def up(h, level, tile):
        return pltpu.make_async_remote_copy(
            src_ref=full.at[tile, span(h, level + 1), :], dst_ref=full.at[tile, span(h, level + 1), :],
            send_sem=up_send.at[tile, level], recv_sem=up_recv.at[tile, level],
            device_id={"col": flip(col, order[h][level])}, device_id_type=MESH)

    def multiply(block, j):
        pair = [(block * CORES + c) * tiles + j for c in range(CORES)]
        hop((block * CORES + (CORES - 1) - core) * tiles + j, twin_send, twin).wait_recv()
        right = jnp.concatenate([gath[tile] for tile in pair], axis=1)
        value = jnp.dot(masked[...], right, preferred_element_type=jnp.float32).astype(jnp.bfloat16)
        for h, tile in enumerate(pair):
            part[tile] = value[:, h * TILE:(h + 1) * TILE]
            down(h, 0, tile).start()

    def advance(stage, block, j):
        for h in range(CORES):
            tile = (block * CORES + h) * tiles + j
            if stage < levels:
                down(h, stage, tile).wait_recv()
                keep = span(h, stage + 1)
                value = part[tile, keep, :].astype(jnp.float32) + landed[tile, slot(stage), :].astype(jnp.float32)
                if stage < levels - 1:
                    part[tile, keep, :] = value.astype(jnp.bfloat16)
                    down(h, stage + 1, tile).start()
                else:
                    full[tile, keep, :] = value.astype(jnp.bfloat16)
                    up(h, stage, tile).start()
            else:
                level = 2 * levels - 1 - stage
                up(h, level, tile).wait_recv()
                if level > 0:
                    up(h, level - 1, tile).start()

    def sides(n, behind, action):
        at = n - behind
        step, j = 1 + at // tiles, lax.rem(at, tiles)
        inside = (at >= 0) & (at < units)

        @pl.when((at >= 0) & (at < tiles))
        def _():
            action(z, at)

        @pl.when(inside & (z - step >= 0))
        def _():
            action(z - step, j)

        @pl.when(inside & (z + step < nz))
        def _():
            action(z + step, j)

    def forward(n):
        step, j = 1 + n // tiles, lax.rem(n, tiles)
        from_left = ((z - step) * CORES + core) * tiles + j
        from_right = ((z + step) * CORES + core) * tiles + j

        @pl.when((n < units) & (z - step >= 0))
        def _():
            hop(from_left, right_send, twin).wait_recv()

            @pl.when(has_right)
            def _():
                hop(from_left, right_send, row + CORES).start()

            hop(from_left, twin_send, twin).start()

        @pl.when((n < units) & (z + step < nz))
        def _():
            hop(from_right, left_send, twin).wait_recv()

            @pl.when(has_left)
            def _():
                hop(from_right, left_send, row - CORES).start()

            hop(from_right, twin_send, twin).start()

    @pl.loop(0, units + INNER_LAG * 2 * levels + 1)
    def _(n):
        forward(n)
        sides(n, 0, multiply)
        for stage in list(range(1, 2 * levels, 2)) + list(range(0, 2 * levels, 2)):
            at_end = (stage + 1) // 2
            behind = at_end + (INNER_LAG * (stage + 1) - at_end) * inner
            sides(n, behind, functools.partial(advance, stage))

    for t in range(per_col):
        out[:, t * TILE:(t + 1) * TILE] = full[owner[col * per_col + t]]

    @pl.loop(0, nz * tiles)
    def _(n):
        other, j = n // tiles, lax.rem(n, tiles)
        for h in range(CORES):
            tile = (other * CORES + h) * tiles + j
            for level in range(levels):
                down(h, level, tile).wait_send()
                up(h, level, tile).wait_send()
        mine = (other * CORES + core) * tiles + j
        hop(mine, twin_send, twin).wait_send()

        @pl.when(has_right & (other <= z))
        def _():
            hop(mine, right_send, twin).wait_send()

        @pl.when(has_left & (other >= z))
        def _():
            hop(mine, left_send, twin).wait_send()


def on_device(nrow, ncol, amplitudes, integrals, amp_occupancy, int_occupancy, owner_map):
    rows, depth = amplitudes.shape
    tiles_all = nrow * integrals.shape[1] // TILE
    width = tiles_all * TILE // ncol
    vmem = pl.BlockSpec(memory_space=pltpu.VMEM)
    smem = pl.BlockSpec(memory_space=pltpu.SMEM)
    levels = ncol.bit_length() - 1
    return pl.pallas_call(
        functools.partial(kernel, nrow, ncol),
        out_shape=jax.ShapeDtypeStruct((rows, width), jnp.bfloat16),
        in_specs=[smem, smem, smem, vmem, vmem],
        out_specs=vmem,
        scratch_shapes=[
            pltpu.VMEM((rows, depth), jnp.bfloat16),
            pltpu.VMEM((tiles_all, depth, TILE), jnp.bfloat16),
            pltpu.VMEM((tiles_all, rows, TILE), jnp.bfloat16),
            pltpu.VMEM((tiles_all, rows, TILE), jnp.bfloat16),
            pltpu.VMEM((tiles_all, rows, TILE), jnp.bfloat16),
            pltpu.SemaphoreType.DMA((tiles_all,)),
            pltpu.SemaphoreType.DMA((tiles_all,)),
            pltpu.SemaphoreType.DMA((tiles_all,)),
            pltpu.SemaphoreType.DMA((tiles_all,)),
            pltpu.SemaphoreType.DMA((tiles_all, levels)),
            pltpu.SemaphoreType.DMA((tiles_all, levels)),
            pltpu.SemaphoreType.DMA((tiles_all, levels)),
            pltpu.SemaphoreType.DMA((tiles_all, levels)),
        ],
        compiler_params=pltpu.CompilerParams(
            collective_id=0, has_side_effects=True, vmem_limit_bytes=48 * 1024 * 1024),
        cost_estimate=pl.CostEstimate(
            flops=2 * rows * depth * tiles_all * TILE, bytes_accessed=4 * rows * depth * 2, transcendentals=0),
    )(amp_occupancy, int_occupancy, owner_map, amplitudes, integrals)


def solution(mesh):
    placed = (P("row", "col"), P("col", "row"), P("row", "col"), P("col", "row"), P())
    body = functools.partial(on_device, mesh.shape["row"], mesh.shape["col"])
    return jax.shard_map(body, mesh=mesh, in_specs=placed, out_specs=P("row", "col"), check_vma=False)
```

```python
import functools

import jax
import jax.numpy as jnp
from jax import lax
from jax.experimental import pallas as pl
from jax.experimental.pallas import tpu as pltpu
from jax.sharding import PartitionSpec as P

TILE = 128
CORES = 2
END_LAG, INNER_LAG = 1, 2
MESH = pl.DeviceIdType.MESH


def flip(value, mask):
    bit, out = 1, value
    while bit <= mask:
        if mask & bit:
            out = out + bit - 2 * bit * (lax.rem(value // bit, 2))
        bit *= 2
    return out


def orders(ncol):
    bits = [1 << i for i in range(ncol.bit_length() - 1)]
    return (bits, bits[::-1])


def kernel(nrow, ncol, amp_occ, int_occ, owner, amp, integ, out,
           masked, gath, part, landed, full, recv, right_send, left_send, twin_send,
           down_send, down_recv, up_send, up_recv):
    nz = nrow // CORES
    row, col = lax.axis_index("row"), lax.axis_index("col")
    z, core = row // CORES, lax.rem(row, CORES)
    twin = z * CORES + (CORES - 1) - core
    has_left, has_right = z > 0, z < nz - 1
    tiles = integ.shape[1] // TILE
    ktiles = integ.shape[0] // TILE
    nrows = amp.shape[0]
    width = out.shape[1]
    per_col = width // TILE
    order = orders(ncol)

    barrier = pltpu.get_barrier_semaphore()
    pl.semaphore_signal(barrier, inc=1, device_id={"row": twin}, device_id_type=MESH)
    for bit in order[0]:
        pl.semaphore_signal(barrier, inc=1, device_id={"col": flip(col, bit)}, device_id_type=MESH)

    @pl.when(has_left)
    def _():
        pl.semaphore_signal(barrier, inc=1, device_id={"row": row - CORES}, device_id_type=MESH)

    @pl.when(has_right)
    def _():
        pl.semaphore_signal(barrier, inc=1, device_id={"row": row + CORES}, device_id_type=MESH)

    def mask_int(j):
        for k in range(ktiles):
            scale = int_occ[k, j].astype(jnp.float32)
            block = integ[k * TILE:(k + 1) * TILE, j * TILE:(j + 1) * TILE].astype(jnp.float32) * scale
            gath[row * tiles + j, k * TILE:(k + 1) * TILE, :] = block.astype(jnp.bfloat16)

    mask_int(0)
    pl.semaphore_wait(barrier, 1 + len(order[0]) + has_left.astype(jnp.int32) + has_right.astype(jnp.int32))

    def hop(tile, send, target):
        return pltpu.make_async_remote_copy(
            src_ref=gath.at[tile], dst_ref=gath.at[tile], send_sem=send.at[tile],
            recv_sem=recv.at[tile], device_id={"row": target}, device_id_type=MESH)

    for j in range(tiles):
        if j > 0:
            mask_int(j)
        mine = row * tiles + j

        @pl.when(has_right)
        def _():
            hop(mine, right_send, row + CORES).start()

        @pl.when(has_left)
        def _():
            hop(mine, left_send, row - CORES).start()

        hop(mine, twin_send, twin).start()

    for i in range(nrows // TILE):
        for k in range(ktiles):
            scale = amp_occ[i, k].astype(jnp.float32)
            block = amp[i * TILE:(i + 1) * TILE, k * TILE:(k + 1) * TILE].astype(jnp.float32) * scale
            masked[i * TILE:(i + 1) * TILE, k * TILE:(k + 1) * TILE] = block.astype(jnp.bfloat16)

    levels = len(order[0])
    units = (nz - 1) * tiles
    inner = has_left.astype(jnp.int32) * has_right.astype(jnp.int32)
    lag = END_LAG + (INNER_LAG - END_LAG) * inner

    def low(h, level):
        at = 0
        for k in range(level):
            at = at + lax.rem(col // order[h][k], 2) * (nrows >> (k + 1))
        return at

    def span(h, level):
        return pl.ds(pl.multiple_of(low(h, level), nrows >> level), nrows >> level)

    def slot(level):
        return pl.ds(nrows - (nrows >> level), nrows >> (level + 1))

    def down(h, level, tile):
        size = nrows >> (level + 1)
        start = low(h, level) + (1 - lax.rem(col // order[h][level], 2)) * size
        return pltpu.make_async_remote_copy(
            src_ref=part.at[tile, pl.ds(pl.multiple_of(start, size), size), :],
            dst_ref=landed.at[tile, slot(level), :],
            send_sem=down_send.at[tile, level], recv_sem=down_recv.at[tile, level],
            device_id={"col": flip(col, order[h][level])}, device_id_type=MESH)

    def up(h, level, tile):
        return pltpu.make_async_remote_copy(
            src_ref=full.at[tile, span(h, level + 1), :], dst_ref=full.at[tile, span(h, level + 1), :],
            send_sem=up_send.at[tile, level], recv_sem=up_recv.at[tile, level],
            device_id={"col": flip(col, order[h][level])}, device_id_type=MESH)

    def multiply(block, j):
        pair = [(block * CORES + c) * tiles + j for c in range(CORES)]
        hop((block * CORES + (CORES - 1) - core) * tiles + j, twin_send, twin).wait_recv()
        right = jnp.concatenate([gath[tile] for tile in pair], axis=1)
        value = jnp.dot(masked[...], right, preferred_element_type=jnp.float32).astype(jnp.bfloat16)
        for h, tile in enumerate(pair):
            part[tile] = value[:, h * TILE:(h + 1) * TILE]
            down(h, 0, tile).start()

    def advance(stage, block, j):
        for h in range(CORES):
            tile = (block * CORES + h) * tiles + j
            if stage < levels:
                down(h, stage, tile).wait_recv()
                keep = span(h, stage + 1)
                value = part[tile, keep, :].astype(jnp.float32) + landed[tile, slot(stage), :].astype(jnp.float32)
                if stage < levels - 1:
                    part[tile, keep, :] = value.astype(jnp.bfloat16)
                    down(h, stage + 1, tile).start()
                else:
                    full[tile, keep, :] = value.astype(jnp.bfloat16)
                    up(h, stage, tile).start()
            else:
                level = 2 * levels - 1 - stage
                up(h, level, tile).wait_recv()
                if level > 0:
                    up(h, level - 1, tile).start()

    def sides(n, behind, action):
        at = n - behind
        step, j = 1 + at // tiles, lax.rem(at, tiles)
        inside = (at >= 0) & (at < units)

        @pl.when((at >= 0) & (at < tiles))
        def _():
            action(z, at)

        @pl.when(inside & (z - step >= 0))
        def _():
            action(z - step, j)

        @pl.when(inside & (z + step < nz))
        def _():
            action(z + step, j)

    def forward(n):
        step, j = 1 + n // tiles, lax.rem(n, tiles)
        from_left = ((z - step) * CORES + core) * tiles + j
        from_right = ((z + step) * CORES + core) * tiles + j

        @pl.when((n < units) & (z - step >= 0))
        def _():
            hop(from_left, right_send, twin).wait_recv()

            @pl.when(has_right)
            def _():
                hop(from_left, right_send, row + CORES).start()

            hop(from_left, twin_send, twin).start()

        @pl.when((n < units) & (z + step < nz))
        def _():
            hop(from_right, left_send, twin).wait_recv()

            @pl.when(has_left)
            def _():
                hop(from_right, left_send, row - CORES).start()

            hop(from_right, twin_send, twin).start()

    @pl.loop(0, units + INNER_LAG * 2 * levels + 2)
    def _(n):
        forward(n)
        sides(n, 0, multiply)
        for stage in range(2 * levels):
            sides(n, lag * (stage + 1) + inner, functools.partial(advance, stage))

    for t in range(per_col):
        out[:, t * TILE:(t + 1) * TILE] = full[owner[col * per_col + t]]

    @pl.loop(0, nz * tiles)
    def _(n):
        other, j = n // tiles, lax.rem(n, tiles)
        for h in range(CORES):
            tile = (other * CORES + h) * tiles + j
            for level in range(levels):
                down(h, level, tile).wait_send()
                up(h, level, tile).wait_send()
        mine = (other * CORES + core) * tiles + j
        hop(mine, twin_send, twin).wait_send()

        @pl.when(has_right & (other <= z))
        def _():
            hop(mine, right_send, twin).wait_send()

        @pl.when(has_left & (other >= z))
        def _():
            hop(mine, left_send, twin).wait_send()


def on_device(nrow, ncol, amplitudes, integrals, amp_occupancy, int_occupancy, owner_map):
    rows, depth = amplitudes.shape
    tiles_all = nrow * integrals.shape[1] // TILE
    width = tiles_all * TILE // ncol
    vmem = pl.BlockSpec(memory_space=pltpu.VMEM)
    smem = pl.BlockSpec(memory_space=pltpu.SMEM)
    levels = ncol.bit_length() - 1
    return pl.pallas_call(
        functools.partial(kernel, nrow, ncol),
        out_shape=jax.ShapeDtypeStruct((rows, width), jnp.bfloat16),
        in_specs=[smem, smem, smem, vmem, vmem],
        out_specs=vmem,
        scratch_shapes=[
            pltpu.VMEM((rows, depth), jnp.bfloat16),
            pltpu.VMEM((tiles_all, depth, TILE), jnp.bfloat16),
            pltpu.VMEM((tiles_all, rows, TILE), jnp.bfloat16),
            pltpu.VMEM((tiles_all, rows, TILE), jnp.bfloat16),
            pltpu.VMEM((tiles_all, rows, TILE), jnp.bfloat16),
            pltpu.SemaphoreType.DMA((tiles_all,)),
            pltpu.SemaphoreType.DMA((tiles_all,)),
            pltpu.SemaphoreType.DMA((tiles_all,)),
            pltpu.SemaphoreType.DMA((tiles_all,)),
            pltpu.SemaphoreType.DMA((tiles_all, levels)),
            pltpu.SemaphoreType.DMA((tiles_all, levels)),
            pltpu.SemaphoreType.DMA((tiles_all, levels)),
            pltpu.SemaphoreType.DMA((tiles_all, levels)),
        ],
        compiler_params=pltpu.CompilerParams(
            collective_id=0, has_side_effects=True, vmem_limit_bytes=48 * 1024 * 1024),
        cost_estimate=pl.CostEstimate(
            flops=2 * rows * depth * tiles_all * TILE, bytes_accessed=4 * rows * depth * 2, transcendentals=0),
    )(amp_occupancy, int_occupancy, owner_map, amplitudes, integrals)


def solution(mesh):
    placed = (P("row", "col"), P("col", "row"), P("row", "col"), P("col", "row"), P())
    body = functools.partial(on_device, mesh.shape["row"], mesh.shape["col"])
    return jax.shard_map(body, mesh=mesh, in_specs=placed, out_specs=P("row", "col"), check_vma=False)
```
